256 devices in a mesh: pitch: 16 (over z, core), span: 16 (over y, x).
Axes of the slice: x: 4, y: 4, z: 8, core: 2. Of those that a mesh axis runs over, the one named last changes fastest.
Arguments:
- blocks: bfloat16 [16384, 80, 880], P(('pitch', 'span'))
- columns: int32 [16384, 11], P(('pitch', 'span')), may hold values from 0 to 95, as said below
- margin_columns: int32 [8192, 4], P(('pitch', 'span')), may hold values from 0 to 96, as said below
- send_lists: int32 [1024, 8], P(('pitch', 'span')), may hold values from 0 to 63, as said below
- basis: bfloat16 [8, 16384, 80], P(None, ('pitch', 'span')), as said below
Outputs:
- new_vector: bfloat16 [16384, 80], P(('pitch', 'span'))
- projections: float32 [9], replicated
The draws below stay inside these ranges and needn't reach their ends.
Inputs may be any that keep to these rules, and one draw needn't show every extreme that they name: `columns`: slot 0 of each face's row is the face's own index among its subdomain's 64 faces; the other slots hold distinct indices into the intersected subdomain, all different from the face's own index. `margin_columns`: slot 0 of margin face g's row is its own position 64 + g; the other slots hold distinct positions in the intersected subdomain other than its own, or 96 for a dropped coupling. `send_lists`: each row holds 8 distinct faces of its subdomain. `basis`: the vectors are orthonormal under <a, b> up to bfloat16 rounding.
All inputs are finite; a program needn't handle non-finite values.
Results may differ from the reference program's by a relative error of at most 0.03.
The reference program's roundings to bfloat16 on the way (of `precond`) count: a program that leaves them out, or rounds other values in their place, can miss the bound.
Values may be sent and summed in bfloat16 or wider, within the bound.
No kernel may reach another device: no remote copies, remote signals or barrier semaphores. Data moves between devices by JAX's collectives and lax.ppermute only.
A program may use at most 128 MiB of HBM per device.

```python
import math
import jax
import jax.numpy as jnp
from jax import lax

BLOCK = 80
SLOTS = 11
GSLOTS = 4
F_DEV = 64
KRYLOV = 8
SWEEPS = 4
LIST = 8
EXTENDED = 96
NFACES = 16384
LISTS = 1024
MARGINS = 8192
N_PITCH = 16
N_SPAN = 16


def draw_blocks(key, part):
    key = jax.random.fold_in(key, 11)
    spread = 0.4 / math.sqrt(SLOTS * BLOCK)
    noise = jax.random.normal(key, (NFACES, BLOCK, SLOTS * BLOCK), jnp.float32) * spread
    return (noise + jnp.eye(BLOCK, SLOTS * BLOCK, dtype=jnp.float32)).astype(jnp.bfloat16)


def draw_columns(key, part):
    key = jax.random.fold_in(key, 12)
    subkeys = jax.random.split(key, NFACES)
    chosen = jax.vmap(lambda single: jax.random.permutation(single, EXTENDED - 1)[:SLOTS - 1])(subkeys).astype(jnp.int32)
    own_index = (jnp.arange(NFACES, dtype=jnp.int32) % F_DEV)[:, None]
    others = chosen + (chosen >= own_index).astype(jnp.int32)
    return jnp.concatenate([own_index, others], axis=1).astype(jnp.int32)


def draw_margin_columns(key, part):
    key = jax.random.fold_in(key, 15)
    first, second = jax.random.split(key, 2)
    subkeys = jax.random.split(first, MARGINS)
    chosen = jax.vmap(lambda single: jax.random.permutation(single, EXTENDED - 1)[:GSLOTS - 1])(subkeys).astype(jnp.int32)
    own_index = (F_DEV + jnp.arange(MARGINS, dtype=jnp.int32) % (4 * LIST))[:, None]
    others = chosen + (chosen >= own_index).astype(jnp.int32)
    dropped = jax.random.randint(second, (MARGINS, GSLOTS - 1), 0, 3) == 0
    row_ids = lax.broadcasted_iota(jnp.int32, (MARGINS, GSLOTS - 1), 0)
    slot_ids = lax.broadcasted_iota(jnp.int32, (MARGINS, GSLOTS - 1), 1)
    dropped = dropped | (row_ids == 0) & (slot_ids == GSLOTS - 2)
    others = jnp.where(dropped, EXTENDED, others)
    return jnp.concatenate([own_index, others], axis=1).astype(jnp.int32)


def draw_send_lists(key, part):
    key = jax.random.fold_in(key, 13)
    subkeys = jax.random.split(key, LISTS)
    chosen = jax.vmap(lambda single: jax.random.permutation(single, F_DEV)[:LIST])(subkeys)
    return chosen.astype(jnp.int32)


def draw_basis(key, part):
    key = jax.random.fold_in(key, 14)
    first, second, third = jax.random.split(key, 3)
    position = jnp.arange(NFACES, dtype=jnp.float32) / NFACES
    rising = jnp.exp(math.log(3.0) * position)[None, :, None]
    mixing = jax.random.uniform(third, (KRYLOV, 1, 1), jnp.float32, 0.3, 0.8)
    common = jax.random.normal(first, (1, NFACES, BLOCK), jnp.float32)
    separate = jax.random.normal(second, (KRYLOV, NFACES, BLOCK), jnp.float32)
    vectors = (mixing * common + jnp.sqrt(1.0 - mixing * mixing) * separate) * rising
    count = NFACES * BLOCK
    finished = []
    for index in range(KRYLOV):
        current = vectors[index]
        for earlier in finished:
            current = current - jnp.sum(earlier * current) / count * earlier
        current = current / jnp.sqrt(jnp.sum(current * current) / count)
        finished.append(current)
    return jnp.stack(finished, axis=0).astype(jnp.bfloat16)


def setup_inputs(seed: int = 0) -> dict:
    key_of = jax.random.split(jax.random.key(seed), 6)
    return {
        "blocks": draw_blocks(jax.random.fold_in(key_of[5], 71), 0),
        "columns": draw_columns(jax.random.fold_in(key_of[5], 71), 0),
        "margin_columns": draw_margin_columns(jax.random.fold_in(key_of[5], 71), 0),
        "send_lists": draw_send_lists(jax.random.fold_in(key_of[5], 71), 0),
        "basis": draw_basis(jax.random.fold_in(key_of[5], 71), 0),
    }


center_value = 1.0
half_width = 0.5
epsilon = 1e-06

def listed(values, send_rows):
    return jax.vmap(lambda source, chosen: source[chosen])(values, send_rows)

def ghosts(outgoing):
    shaped = outgoing.reshape((N_PITCH, N_SPAN) + outgoing.shape[1:])
    from_lower = jnp.roll(shaped[:, :, 0], 1, axis=0)
    from_upper = jnp.roll(shaped[:, :, 1], -1, axis=0)
    zero_column = jnp.zeros_like(shaped[:, :1, 2])
    from_left = jnp.concatenate([zero_column, shaped[:, :-1, 2]], axis=1)
    from_right = jnp.concatenate([shaped[:, 1:, 3], zero_column], axis=1)
    stacked = jnp.stack([from_lower, from_upper, from_left, from_right], axis=2)
    return stacked.reshape((N_PITCH * N_SPAN, 4 * LIST) + outgoing.shape[3:])

def own_product(block_rows, column_ids, extended):

    def single(entries):
        rows_here, ids_here, vector_here = entries
        gathered = vector_here[ids_here].reshape(F_DEV, SLOTS * BLOCK).astype(jnp.float32)
        return jnp.einsum('fij,fj->fi', rows_here.astype(jnp.float32), gathered, precision=lax.Precision.HIGHEST)
    return lax.map(single, (block_rows, column_ids, extended))

def margin_product(margin_rows, margin_ids, padded):

    def single(entries):
        rows_here, ids_here, vector_here = entries
        gathered = vector_here[ids_here].reshape(4 * LIST, GSLOTS * BLOCK).astype(jnp.float32)
        return jnp.einsum('gij,gj->gi', rows_here.astype(jnp.float32), gathered, precision=lax.Precision.HIGHEST)
    return lax.map(single, (margin_rows, margin_ids, padded))

def reference(blocks, columns, margin_columns, send_lists, basis):
    subdomains = N_PITCH * N_SPAN
    block_rows = blocks.reshape(subdomains, F_DEV, BLOCK, SLOTS * BLOCK)
    column_ids = columns.reshape(subdomains, F_DEV, SLOTS)
    margin_ids = margin_columns.reshape(subdomains, 4 * LIST, GSLOTS)
    send_rows = send_lists.reshape(subdomains, 4, LIST)
    latest = basis[KRYLOV - 1].reshape(subdomains, F_DEV, BLOCK)
    margin_rows = ghosts(listed(block_rows[:, :, :, :GSLOTS * BLOCK], send_rows))
    ghost_values = ghosts(listed(latest, send_rows))
    residual = jnp.concatenate([latest, ghost_values], axis=1).astype(jnp.float32)
    stretch = center_value / half_width
    ratio_now = 1.0 / stretch
    direction = residual / center_value
    solution = jnp.zeros_like(residual)
    zero_row = jnp.zeros((subdomains, 1, BLOCK), jnp.bfloat16)
    for sweep_index in range(SWEEPS):
        solution = solution + direction
        if sweep_index < SWEEPS - 1:
            rounded = direction.astype(jnp.bfloat16)
            padded = jnp.concatenate([rounded, zero_row], axis=1)
            applied = jnp.concatenate([own_product(block_rows, column_ids, rounded), margin_product(margin_rows, margin_ids, padded)], axis=1)
            residual = residual - applied
            ratio_next = 1.0 / (2.0 * stretch - ratio_now)
            direction = ratio_next * ratio_now * direction + 2.0 * ratio_next / half_width * residual
            ratio_now = ratio_next
    precond = solution[:, :F_DEV].astype(jnp.bfloat16)
    extended = jnp.concatenate([precond, ghosts(listed(precond, send_rows))], axis=1)
    image = own_product(block_rows, column_ids, extended).reshape(NFACES, BLOCK)
    inverse_count = 1.0 / (NFACES * BLOCK)
    basis_wide = basis.astype(jnp.float32)
    heights = lax.optimization_barrier(jnp.sum(basis_wide * image[None], axis=(1, 2))) * inverse_count
    remainder = image - jnp.tensordot(heights, basis_wide, axes=1, precision=lax.Precision.HIGHEST)
    length_value = jnp.sqrt(jnp.sum(remainder * remainder) * inverse_count + epsilon)
    new_vector = (remainder / length_value).astype(jnp.bfloat16)
    return (new_vector, jnp.concatenate([heights, length_value[None]]))
```

```python
import functools

import jax
import jax.numpy as jnp
from jax import lax
from jax.experimental import pallas as pl
from jax.experimental.pallas import tpu as pltpu
from jax.sharding import PartitionSpec as P

BLOCK = 80
SLOTS = 11
GSLOTS = 4
F_DEV = 64
KRYLOV = 8
SWEEPS = 4
LIST = 8
LANES = 128
WIDTH = SLOTS * BLOCK
LEAD = 384
KTILES = ((0, 256), (256, 512), (512, 768), (768, 880))

center_value = 1.0
half_width = 0.5
epsilon = 1e-06

f32 = jnp.float32
bf16 = jnp.bfloat16
VMEM = pl.BlockSpec(memory_space=pltpu.VMEM)
SMEM = pl.BlockSpec(memory_space=pltpu.SMEM)
ANY = pl.BlockSpec(memory_space=pl.ANY)
PARAMS = pltpu.CompilerParams(vmem_limit_bytes=48 * 2**20)


def sweep_constants():
    stretch = center_value / half_width
    ratio_now = 1.0 / stretch
    factors = []
    for _ in range(SWEEPS - 1):
        ratio_next = 1.0 / (2.0 * stretch - ratio_now)
        factors.append((ratio_next * ratio_now, 2.0 * ratio_next / half_width))
        ratio_now = ratio_next
    return factors


def shifted(value, axis, by, wrap):
    devices = lax.axis_size(axis)
    pairs = [(i, (i + by) % devices) for i in range(devices) if wrap or 0 <= i + by < devices]
    return lax.ppermute(value, axis, pairs)


def exchange(outgoing):
    return [
        shifted(outgoing[0], "pitch", 1, True),
        shifted(outgoing[1], "pitch", -1, True),
        shifted(outgoing[2], "span", 1, False),
        shifted(outgoing[3], "span", -1, False),
    ]


def lane_ids():
    return lax.broadcasted_iota(jnp.int32, (BLOCK, LANES), 1)


def fill_columns(columns_ref, margin_ref, ids):
    ids[...] = jnp.full(ids.shape, LANES - 1, jnp.int32)
    ids[0:SLOTS, 0:F_DEV] = columns_ref[...]
    if margin_ref is not None:
        ids[0:GSLOTS, F_DEV : F_DEV + 4 * LIST] = margin_ref[...]


def fill_gathered(vector, ids, gathered):
    rows = lax.broadcasted_iota(jnp.int32, (LANES, LANES), 0)
    for slot in range(SLOTS):
        chosen = (rows == ids[slot : slot + 1, :]).astype(f32).astype(bf16)
        part = jnp.dot(vector, chosen, preferred_element_type=f32)
        gathered[slot * BLOCK : (slot + 1) * BLOCK, :] = part.astype(bf16)


def own_product(rows_ref, gathered, wait):
    lanes = lane_ids()
    total = jnp.zeros((BLOCK, LANES), f32)
    for index, (start, stop) in enumerate(KTILES):
        wait(index)
        rows = rows_ref[:, :, start:stop].reshape(F_DEV * BLOCK, stop - start)
        product = jnp.dot(rows, gathered[start:stop, :], preferred_element_type=f32)
        part = jnp.zeros((BLOCK, LANES), f32)
        for face in range(F_DEV):
            part = jnp.where(lanes == face, product[face * BLOCK : (face + 1) * BLOCK], part)
        total = total + part
    return total


def margin_product(row_refs, gathered):
    lanes = lane_ids()
    total = jnp.zeros((BLOCK, LANES), f32)
    for start, stop in ((0, 256), (256, LEAD)):
        part = jnp.zeros((BLOCK, LANES), f32)
        for index, ref in enumerate(row_refs):
            rows = ref[:, :, start:stop].reshape(LIST * BLOCK, stop - start)
            product = jnp.dot(rows, gathered[start:stop, :], preferred_element_type=f32)
            for face in range(LIST):
                lane = F_DEV + index * LIST + face
                part = jnp.where(lanes == lane, product[face * BLOCK : (face + 1) * BLOCK], part)
        total = total + part
    return total


def stage_rows(rows_hbm, rows_ref, sems):
    copies = []
    for index, (start, stop) in enumerate(KTILES):
        copy = pltpu.make_async_copy(
            rows_hbm.at[:, :, start:stop], rows_ref.at[:, :, start:stop], sems.at[index]
        )
        copy.start()
        copies.append(copy)
    return copies


def values_kernel(lists, latest, out0, out1, out2, out3, wide):
    wide[:, 0:BLOCK] = latest[...].astype(f32)
    wide[:, BLOCK:LANES] = jnp.zeros((F_DEV, LANES - BLOCK), f32)
    for index, out in enumerate((out0, out1, out2, out3)):
        for face in range(LIST):
            out[face : face + 1, :] = wide[pl.ds(lists[index, face], 1), :]


def rows_kernel(lists, rows, out0, out1, out2, out3, sem):
    copies = []
    for index, out in enumerate((out0, out1, out2, out3)):
        for face in range(LIST):
            copy = pltpu.make_async_copy(
                rows.at[lists[index, face], :, pl.ds(0, LEAD)], out.at[face], sem.at[index * LIST + face]
            )
            copy.start()
            copies.append(copy)
    for copy in copies:
        copy.wait()


def first_kernel(rows_hbm, columns, latest, g0, g1, g2, g3, residual_out, applied_out, rows, sems, wide, ids, gathered):
    copies = stage_rows(rows_hbm, rows, sems)
    fill_columns(columns, None, ids)
    wide[...] = jnp.zeros((LANES, LANES), f32)
    wide[0:F_DEV, 0:BLOCK] = latest[...].astype(f32)
    for index, ghost in enumerate((g0, g1, g2, g3)):
        start = F_DEV + index * LIST
        wide[start : start + LIST, :] = ghost[...]
    residual = wide[...].T[0:BLOCK]
    residual_out[...] = residual
    fill_gathered((residual / center_value).astype(bf16), ids, gathered)
    applied_out[...] = own_product(rows, gathered, lambda index: copies[index].wait())


def sweeps_kernel(
    rows_hbm, columns, margin_columns, lists, residual_in, applied_in, m0, m1, m2, m3,
    precond_out, out0, out1, out2, out3, rows, sems, wide, ids, gathered,
):
    copies = stage_rows(rows_hbm, rows, sems)
    fill_columns(columns, margin_columns, ids)
    factors = sweep_constants()
    margins = (m0, m1, m2, m3)
    residual = residual_in[...]
    direction = residual / center_value
    solution = direction
    for sweep in range(SWEEPS - 1):
        fill_gathered(direction.astype(bf16), ids, gathered)
        if sweep == 0:
            applied = applied_in[...]
        elif sweep == 1:
            applied = own_product(rows, gathered, lambda index: copies[index].wait())
        else:
            applied = own_product(rows, gathered, lambda index: None)
        if sweep < SWEEPS - 2:
            applied = applied + margin_product(margins, gathered)
        residual = residual - applied
        keep_factor, push_factor = factors[sweep]
        direction = keep_factor * direction + push_factor * residual
        solution = solution + direction
    own = jnp.where(lane_ids() < F_DEV, solution, 0.0).astype(bf16)
    precond_out[...] = own
    wide[0:BLOCK, :] = own.astype(f32)
    wide[BLOCK:LANES, :] = jnp.zeros((LANES - BLOCK, LANES), f32)
    wide[...] = wide[...].T
    for index, out in enumerate((out0, out1, out2, out3)):
        for face in range(LIST):
            out[face : face + 1, :] = wide[pl.ds(lists[index, face], 1), :]


PAIRS = [(a, b) for a in range(KRYLOV) for b in range(a, KRYLOV)]
SUMS = KRYLOV + 1 + len(PAIRS)


def image_kernel(rows_hbm, columns, precond, g0, g1, g2, g3, basis, image_out, sums_out, rows, sems, wide, ids, gathered, sums):
    copies = stage_rows(rows_hbm, rows, sems)
    fill_columns(columns, None, ids)
    wide[...] = jnp.zeros((LANES, LANES), f32)
    for index, ghost in enumerate((g0, g1, g2, g3)):
        start = F_DEV + index * LIST
        wide[start : start + LIST, :] = ghost[...]
    vector = precond[...] + wide[...].T[0:BLOCK].astype(bf16)
    fill_gathered(vector, ids, gathered)
    sums[...] = jnp.zeros((LANES, LANES), f32)
    spread = [basis[j].astype(f32) for j in range(KRYLOV)]
    for index, (a, b) in enumerate(PAIRS):
        row = KRYLOV + 1 + index
        sums[row : row + 1, 0:BLOCK] = jnp.sum(spread[a] * spread[b], axis=0, keepdims=True)
    product = own_product(rows, gathered, lambda index: copies[index].wait())
    wide[0:BLOCK, :] = product
    wide[BLOCK:LANES, :] = jnp.zeros((LANES - BLOCK, LANES), f32)
    image = wide[...].T[0:F_DEV, 0:BLOCK]
    image_out[...] = image
    for j in range(KRYLOV):
        sums[j : j + 1, 0:BLOCK] = jnp.sum(spread[j] * image, axis=0, keepdims=True)
    sums[KRYLOV : KRYLOV + 1, 0:BLOCK] = jnp.sum(image * image, axis=0, keepdims=True)
    totals = jnp.sum(sums[...], axis=1, keepdims=True)
    row = jnp.broadcast_to(totals, (LANES, LANES)).T[0:1]
    sums_out[...] = jnp.broadcast_to(row, sums_out.shape)


def last_kernel(inverse_count, image, basis, sums, vector_out, projections_out):
    totals = jnp.sum(sums[...], axis=0, keepdims=True) * inverse_count
    entry = lambda index: totals[:, index : index + 1]
    heights = [entry(j) for j in range(KRYLOV)]
    squares = entry(KRYLOV)
    for index, (a, b) in enumerate(PAIRS):
        term = heights[a] * heights[b] * entry(KRYLOV + 1 + index)
        squares = squares + (term if a == b else 2.0 * term)
    for j in range(KRYLOV):
        squares = squares - 2.0 * heights[j] * heights[j]
    length = jnp.sqrt(squares + epsilon)
    remainder = image[...]
    for j in range(KRYLOV):
        remainder = remainder - heights[j] * basis[j].astype(f32)
    vector_out[...] = (remainder / length).astype(bf16)
    lanes = lax.broadcasted_iota(jnp.int32, (1, LANES), 1)
    projections_out[...] = jnp.where(lanes == KRYLOV, length, totals)


def shape(dims, dtype):
    return jax.ShapeDtypeStruct(dims, dtype)


def per_device(blocks, columns, margin_columns, send_lists, basis):
    devices = lax.axis_size("pitch") * lax.axis_size("span")
    latest = basis[KRYLOV - 1]
    columns_t = columns.T
    margin_t = margin_columns.T
    row_scratch = pltpu.VMEM((F_DEV, BLOCK, WIDTH), bf16)
    row_sems = pltpu.SemaphoreType.DMA((len(KTILES),))
    square = pltpu.VMEM((LANES, LANES), f32)
    ids = pltpu.VMEM((16, LANES), jnp.int32)
    gathered = pltpu.VMEM((WIDTH, LANES), bf16)

    values = pl.pallas_call(
        values_kernel,
        out_shape=[shape((LIST, LANES), f32)] * 4,
        in_specs=[SMEM, VMEM],
        out_specs=[VMEM] * 4,
        scratch_shapes=[pltpu.VMEM((F_DEV, LANES), f32)],
        name="pack_values",
    )(send_lists, latest)
    ghosts = exchange(values)
    leading = pl.pallas_call(
        rows_kernel,
        out_shape=[shape((LIST, BLOCK, LEAD), bf16)] * 4,
        in_specs=[SMEM, ANY],
        out_specs=[ANY] * 4,
        scratch_shapes=[pltpu.SemaphoreType.DMA((4 * LIST,))],
        name="pack_rows",
    )(send_lists, blocks)
    margins = exchange(leading)
    residual, applied = pl.pallas_call(
        first_kernel,
        out_shape=[shape((BLOCK, LANES), f32)] * 2,
        in_specs=[ANY] + [VMEM] * 6,
        out_specs=[VMEM] * 2,
        scratch_shapes=[row_scratch, row_sems, square, ids, gathered],
        compiler_params=PARAMS,
        name="first_product",
    )(blocks, columns_t, latest, *ghosts)
    precond, *values = pl.pallas_call(
        sweeps_kernel,
        out_shape=[shape((BLOCK, LANES), bf16)] + [shape((LIST, LANES), f32)] * 4,
        in_specs=[ANY, VMEM, VMEM, SMEM] + [VMEM] * 6,
        out_specs=[VMEM] * 5,
        scratch_shapes=[row_scratch, row_sems, square, ids, gathered],
        compiler_params=PARAMS,
        name="sweeps",
    )(blocks, columns_t, margin_t, send_lists, residual, applied, *margins)
    ghosts = exchange(values)
    image, sums = pl.pallas_call(
        image_kernel,
        out_shape=[shape((F_DEV, BLOCK), f32), shape((devices, LANES), f32)],
        in_specs=[ANY] + [VMEM] * 7,
        out_specs=[VMEM] * 2,
        scratch_shapes=[row_scratch, row_sems, square, ids, gathered, square],
        compiler_params=PARAMS,
        name="image",
    )(blocks, columns_t, precond, *ghosts, basis)
    sums = lax.all_to_all(sums.reshape(devices, 1, LANES), ("pitch", "span"), 0, 0)
    new_vector, projections = pl.pallas_call(
        functools.partial(last_kernel, 1.0 / (devices * F_DEV * BLOCK)),
        out_shape=[shape((F_DEV, BLOCK), bf16), shape((1, LANES), f32)],
        in_specs=[VMEM] * 3,
        out_specs=[VMEM] * 2,
        name="new_vector",
    )(image, basis, sums.reshape(devices, LANES))
    return (new_vector, projections[0, 0 : KRYLOV + 1])


def solution(mesh):
    return jax.shard_map(
        per_device,
        mesh=mesh,
        in_specs=(
            P(("pitch", "span"), None, None),
            P(("pitch", "span"), None),
            P(("pitch", "span"), None),
            P(("pitch", "span"), None),
            P(None, ("pitch", "span"), None),
        ),
        out_specs=(P(("pitch", "span"), None), P()),
        check_vma=False,
    )
```

```python
import functools

import jax
import jax.numpy as jnp
from jax import lax
from jax.experimental import pallas as pl
from jax.experimental.pallas import tpu as pltpu
from jax.sharding import PartitionSpec as P

BLOCK = 80
SLOTS = 11
GSLOTS = 4
F_DEV = 64
KRYLOV = 8
SWEEPS = 4
LIST = 8
LANES = 128
WIDTH = SLOTS * BLOCK
MESSAGE = 208
KTILES = ((0, 256), (256, 512), (512, 768), (768, 880))

center_value = 1.0
half_width = 0.5
epsilon = 1e-06

f32 = jnp.float32
bf16 = jnp.bfloat16
VMEM = pl.BlockSpec(memory_space=pltpu.VMEM)
SMEM = pl.BlockSpec(memory_space=pltpu.SMEM)
ANY = pl.BlockSpec(memory_space=pl.ANY)
PARAMS = pltpu.CompilerParams(vmem_limit_bytes=32 * 2**20)


def sweep_constants():
    stretch = center_value / half_width
    ratio_now = 1.0 / stretch
    factors = []
    for _ in range(SWEEPS - 1):
        ratio_next = 1.0 / (2.0 * stretch - ratio_now)
        factors.append((ratio_next * ratio_now, 2.0 * ratio_next / half_width))
        ratio_now = ratio_next
    return factors


def positions():
    return lax.axis_index("pitch") % 2, lax.axis_index("span") % 2


def sent_lists():
    pitch_odd, span_odd = positions()
    return pitch_odd, 1 - pitch_odd, 2 + span_odd, 3 - span_odd


def received_groups():
    pitch_odd, span_odd = positions()
    return 1 - pitch_odd, pitch_odd, 3 - span_odd, 2 + span_odd


def exchange(outgoing):
    pitch, span = lax.axis_size("pitch"), lax.axis_size("span")
    received = []
    for index, value in enumerate(outgoing):
        axis, devices, wrap = ("pitch", pitch, True) if index < 2 else ("span", span, False)
        first = index % 2
        pairs = []
        for low in range(first, devices, 2):
            high = low + 1
            if high < devices or wrap:
                pairs += [(low, high % devices), (high % devices, low)]
        received.append(lax.ppermute(value, axis, pairs))
    return received


def lane_ids():
    return lax.broadcasted_iota(jnp.int32, (BLOCK, LANES), 1)


def fill_columns(columns_ref, margin_ref, ids):
    ids[...] = jnp.full(ids.shape, LANES - 1, jnp.int32)
    ids[0:SLOTS, 0:F_DEV] = columns_ref[...]
    if margin_ref is not None:
        ids[0:GSLOTS, F_DEV : F_DEV + 4 * LIST] = margin_ref[...]


def fill_gathered(vector, ids, gathered):
    rows = lax.broadcasted_iota(jnp.int32, (LANES, LANES), 0)
    for slot in range(SLOTS):
        chosen = (rows == ids[slot : slot + 1, :]).astype(f32).astype(bf16)
        part = jnp.dot(vector, chosen, preferred_element_type=f32)
        gathered[slot * BLOCK : (slot + 1) * BLOCK, :] = part.astype(bf16)


def own_product(rows_ref, gathered):
    lanes = lane_ids()
    total = jnp.zeros((BLOCK, LANES), f32)
    for start, stop in KTILES:
        rows = rows_ref[:, :, start:stop].reshape(F_DEV * BLOCK, stop - start)
        product = jnp.dot(rows, gathered[start:stop, :], preferred_element_type=f32)
        part = jnp.zeros((BLOCK, LANES), f32)
        for face in range(F_DEV):
            part = jnp.where(lanes == face, product[face * BLOCK : (face + 1) * BLOCK], part)
        total = total + part
    return total


def margin_product(messages, groups, gathered, tail):
    lanes = lane_ids()
    tail[...] = jnp.zeros(tail.shape, bf16)
    tail[0:64, 0:LANES] = gathered[256:320, :]
    tail[64:128, LANES : 2 * LANES] = gathered[256:320, :]
    total = jnp.zeros((BLOCK, LANES), f32)
    ends = jnp.zeros((BLOCK, LANES), f32)
    for message, group in zip(messages, groups):
        rows = jnp.concatenate([message[:, 0:BLOCK, :], message[:, BLOCK : 2 * BLOCK, :]], axis=-1)
        product = jnp.dot(rows.reshape(LIST * BLOCK, 256), gathered[0:256, :], preferred_element_type=f32)
        rest = message[:, 2 * BLOCK : MESSAGE, :].reshape(LIST * 48, LANES)
        second = jnp.dot(rest, tail[...], preferred_element_type=f32)
        for face in range(LIST):
            chosen = lanes == F_DEV + group * LIST + face
            total = jnp.where(chosen, product[face * BLOCK : (face + 1) * BLOCK], total)
            part = second[face * 48 : face * 48 + 40]
            ends = jnp.where(chosen, jnp.concatenate([part[:, 0:LANES], part[:, LANES:]], axis=0), ends)
    return total + ends


def pack_kernel(lists, rows, basis, out0, out1, out2, out3, latest, wide, ends, sem_latest, sems, sem_ends):
    first = pltpu.make_async_copy(basis.at[KRYLOV - 1], latest, sem_latest)
    first.start()
    outs = (out0, out1, out2, out3)
    numbers = sent_lists()
    copies = []
    for index in (2, 3, 1, 0):
        out, number = outs[index], numbers[index]
        for face in range(LIST):
            at = lists[number, face]
            slot = index * LIST + face
            copies.append(pltpu.make_async_copy(rows.at[at, :, pl.ds(256, LANES)], ends.at[slot], sem_ends.at[slot]))
            copies.append(
                pltpu.make_async_copy(rows.at[at, :, pl.ds(0, LANES)], out.at[face, pl.ds(0, BLOCK), :], sems.at[2 * slot])
            )
            copies.append(
                pltpu.make_async_copy(
                    rows.at[at, :, pl.ds(LANES, LANES)], out.at[face, pl.ds(BLOCK, BLOCK), :], sems.at[2 * slot + 1]
                )
            )
            for copy in copies[-3:]:
                copy.start()
    first.wait()
    wide[:, 0:BLOCK] = latest[...].astype(f32)
    wide[:, BLOCK:LANES] = jnp.zeros((F_DEV, LANES - BLOCK), f32)
    lanes = lax.broadcasted_iota(jnp.int32, (40, LANES), 1)
    for copy in copies:
        copy.wait()
    for index, out in enumerate(outs):
        for face in range(LIST):
            end = ends[index * LIST + face].astype(f32)
            both = jnp.where(lanes < 64, end[0:40], pltpu.roll(end[40:80], 64, 1))
            value = jnp.broadcast_to(wide[pl.ds(lists[numbers[index], face], 1), :], (8, LANES))
            out[face, 2 * BLOCK : MESSAGE, :] = jnp.concatenate([both, value], axis=0).astype(bf16)


def sweeps_kernel(
    rows, columns, margin_columns, lists, basis, m0, m1, m2, m3,
    precond_out, out0, out1, out2, out3, wide, ids, gathered, tail,
):
    fill_columns(columns, margin_columns, ids)
    factors = sweep_constants()
    messages, groups = (m0, m1, m2, m3), received_groups()
    wide[...] = jnp.zeros((LANES, LANES), f32)
    wide[0:F_DEV, 0:BLOCK] = basis[KRYLOV - 1].astype(f32)
    for message, group in zip(messages, groups):
        start = pl.multiple_of(F_DEV + group * LIST, LIST)
        last = [message[face, MESSAGE - 16 : MESSAGE, :].astype(f32)[8:9] for face in range(LIST)]
        wide[pl.ds(start, LIST), :] = jnp.concatenate(last, axis=0)
    residual = wide[...].T[0:BLOCK]
    direction = residual / center_value
    solution = direction
    for sweep in range(SWEEPS - 1):
        fill_gathered(direction.astype(bf16), ids, gathered)
        applied = own_product(rows, gathered)
        if sweep < SWEEPS - 2:
            applied = applied + margin_product(messages, groups, gathered, tail)
        residual = residual - applied
        keep_factor, push_factor = factors[sweep]
        direction = keep_factor * direction + push_factor * residual
        solution = solution + direction
    own = jnp.where(lane_ids() < F_DEV, solution, 0.0).astype(bf16)
    precond_out[...] = own
    wide[0:BLOCK, :] = own.astype(f32)
    wide[BLOCK:LANES, :] = jnp.zeros((LANES - BLOCK, LANES), f32)
    wide[...] = wide[...].T
    for out, number in zip((out0, out1, out2, out3), sent_lists()):
        for face in range(LIST):
            out[face : face + 1, :] = wide[pl.ds(lists[number, face], 1), :]


PAIRS = [(a, b) for a in range(KRYLOV) for b in range(a, KRYLOV)]
SUMS = KRYLOV + 1 + len(PAIRS)


def image_kernel(rows, columns, precond, g0, g1, g2, g3, basis, image_out, sums_out, wide, ids, gathered, sums):
    fill_columns(columns, None, ids)
    wide[...] = jnp.zeros((LANES, LANES), f32)
    for ghost, group in zip((g0, g1, g2, g3), received_groups()):
        wide[pl.ds(pl.multiple_of(F_DEV + group * LIST, LIST), LIST), :] = ghost[...]
    vector = precond[...] + wide[...].T[0:BLOCK].astype(bf16)
    fill_gathered(vector, ids, gathered)
    sums[...] = jnp.zeros((LANES, LANES), f32)
    spread = [basis[j].astype(f32) for j in range(KRYLOV)]
    for index, (a, b) in enumerate(PAIRS):
        row = KRYLOV + 1 + index
        sums[row : row + 1, 0:BLOCK] = jnp.sum(spread[a] * spread[b], axis=0, keepdims=True)
    product = own_product(rows, gathered)
    wide[0:BLOCK, :] = product
    wide[BLOCK:LANES, :] = jnp.zeros((LANES - BLOCK, LANES), f32)
    image = wide[...].T[0:F_DEV, 0:BLOCK]
    image_out[...] = image
    for j in range(KRYLOV):
        sums[j : j + 1, 0:BLOCK] = jnp.sum(spread[j] * image, axis=0, keepdims=True)
    sums[KRYLOV : KRYLOV + 1, 0:BLOCK] = jnp.sum(image * image, axis=0, keepdims=True)
    totals = jnp.sum(sums[...], axis=1, keepdims=True)
    row = jnp.broadcast_to(totals, (LANES, LANES)).T[0:1]
    sums_out[...] = jnp.broadcast_to(row, sums_out.shape)


def last_kernel(inverse_count, image, basis, sums, vector_out, projections_out):
    totals = jnp.sum(sums[...], axis=0, keepdims=True) * inverse_count
    entry = lambda index: totals[:, index : index + 1]
    heights = [entry(j) for j in range(KRYLOV)]
    squares = entry(KRYLOV)
    for index, (a, b) in enumerate(PAIRS):
        term = heights[a] * heights[b] * entry(KRYLOV + 1 + index)
        squares = squares + (term if a == b else 2.0 * term)
    for j in range(KRYLOV):
        squares = squares - 2.0 * heights[j] * heights[j]
    length = jnp.sqrt(squares + epsilon)
    remainder = image[...]
    for j in range(KRYLOV):
        remainder = remainder - heights[j] * basis[j].astype(f32)
    vector_out[...] = (remainder / length).astype(bf16)
    lanes = lax.broadcasted_iota(jnp.int32, (1, LANES), 1)
    row = jnp.where(lanes == KRYLOV, length, totals)
    projections_out[...] = row[0, 0 : KRYLOV + 1]


def shape(dims, dtype):
    return jax.ShapeDtypeStruct(dims, dtype)


def per_device(blocks, columns, margin_columns, send_lists, basis):
    devices = lax.axis_size("pitch") * lax.axis_size("span")
    columns_t = columns.T
    margin_t = margin_columns.T
    square = pltpu.VMEM((LANES, LANES), f32)
    ids = pltpu.VMEM((16, LANES), jnp.int32)
    gathered = pltpu.VMEM((WIDTH, LANES), bf16)

    messages = pl.pallas_call(
        pack_kernel,
        out_shape=[shape((LIST, MESSAGE, LANES), bf16)] * 4,
        in_specs=[SMEM, ANY, ANY],
        out_specs=[VMEM] * 4,
        scratch_shapes=[
            pltpu.VMEM((F_DEV, BLOCK), bf16),
            pltpu.VMEM((F_DEV, LANES), f32),
            pltpu.VMEM((4 * LIST, BLOCK, LANES), bf16),
            pltpu.SemaphoreType.DMA,
            pltpu.SemaphoreType.DMA((8 * LIST,)),
            pltpu.SemaphoreType.DMA((4 * LIST,)),
        ],
        compiler_params=PARAMS,
        name="pack",
    )(send_lists, blocks, basis)
    messages = exchange(messages)
    precond, *values = pl.pallas_call(
        sweeps_kernel,
        out_shape=[shape((BLOCK, LANES), bf16)] + [shape((LIST, LANES), f32)] * 4,
        in_specs=[VMEM, VMEM, VMEM, SMEM] + [VMEM] * 5,
        out_specs=[VMEM] * 5,
        scratch_shapes=[square, ids, gathered, pltpu.VMEM((LANES, 2 * LANES), bf16)],
        compiler_params=PARAMS,
        name="sweeps",
    )(blocks, columns_t, margin_t, send_lists, basis, *messages)
    ghosts = exchange(values)
    image, sums = pl.pallas_call(
        image_kernel,
        out_shape=[shape((F_DEV, BLOCK), f32), shape((devices, LANES), f32)],
        in_specs=[VMEM] * 8,
        out_specs=[VMEM] * 2,
        scratch_shapes=[square, ids, gathered, square],
        compiler_params=PARAMS,
        name="image",
    )(blocks, columns_t, precond, *ghosts, basis)
    sums = lax.all_to_all(sums.reshape(devices, 1, LANES), ("pitch", "span"), 0, 0)
    new_vector, projections = pl.pallas_call(
        functools.partial(last_kernel, 1.0 / (devices * F_DEV * BLOCK)),
        out_shape=[shape((F_DEV, BLOCK), bf16), shape((KRYLOV + 1,), f32)],
        in_specs=[VMEM] * 3,
        out_specs=[VMEM] * 2,
        name="new_vector",
    )(image, basis, sums.reshape(devices, LANES))
    return (new_vector, projections)


def solution(mesh):
    return jax.shard_map(
        per_device,
        mesh=mesh,
        in_specs=(
            P(("pitch", "span"), None, None),
            P(("pitch", "span"), None),
            P(("pitch", "span"), None),
            P(("pitch", "span"), None),
            P(None, ("pitch", "span"), None),
        ),
        out_specs=(P(("pitch", "span"), None), P()),
        check_vma=False,
    )
```

```python
import functools

import jax
import jax.numpy as jnp
from jax import lax
from jax.experimental import pallas as pl
from jax.experimental.pallas import tpu as pltpu
from jax.sharding import PartitionSpec as P

BLOCK = 80
SLOTS = 11
GSLOTS = 4
F_DEV = 64
KRYLOV = 8
SWEEPS = 4
LIST = 8
LANES = 128
WIDTH = SLOTS * BLOCK
LEAD = 384
MESSAGE = 208
GRAM = 64
GUARD = 2.0**-11
KTILES = ((0, 256), (256, 512), (512, 768), (768, 880))
REST = 768
SPLIT = 24

center_value = 1.0
half_width = 0.5
epsilon = 1e-06

f32 = jnp.float32
bf16 = jnp.bfloat16
VMEM = pl.BlockSpec(memory_space=pltpu.VMEM)
SMEM = pl.BlockSpec(memory_space=pltpu.SMEM)
ANY = pl.BlockSpec(memory_space=pl.ANY)
PARAMS = pltpu.CompilerParams(vmem_limit_bytes=32 * 2**20)
PACK_PARAMS = pltpu.CompilerParams(vmem_limit_bytes=58 * 2**20)


def sweep_constants():
    stretch = center_value / half_width
    ratio_now = 1.0 / stretch
    factors = []
    for _ in range(SWEEPS - 1):
        ratio_next = 1.0 / (2.0 * stretch - ratio_now)
        factors.append((ratio_next * ratio_now, 2.0 * ratio_next / half_width))
        ratio_now = ratio_next
    return factors


def positions():
    return lax.axis_index("pitch") % 2, lax.axis_index("span") % 2


def sent_lists():
    pitch_odd, span_odd = positions()
    return pitch_odd, 1 - pitch_odd, 2 + span_odd, 3 - span_odd


def received_groups():
    pitch_odd, span_odd = positions()
    span = lax.axis_index("span")
    inside = (span != 0) & (span != lax.axis_size("span") - 1)
    return (1 - pitch_odd, True), (pitch_odd, True), (3 - span_odd, True), (2 + span_odd, inside)


def exchange(outgoing):
    received = [None] * 4
    for index in (3, 2, 1, 0):
        axis = "pitch" if index < 2 else "span"
        devices = lax.axis_size(axis)
        pairs = []
        for low in range(index % 2, devices, 2):
            high = (low + 1) % devices
            pairs += [(low, high), (high, low)]
        received[index] = lax.ppermute(outgoing[index], axis, pairs)
    return received


def lane_ids():
    return lax.broadcasted_iota(jnp.int32, (BLOCK, LANES), 1)


def choose_kernel(rows, columns, margin_columns, chosen, ids):
    ids[...] = jnp.full(ids.shape, LANES - 1, jnp.int32)
    ids[0:SLOTS, 0:F_DEV] = columns[...]
    ids[0:GSLOTS, F_DEV : F_DEV + 4 * LIST] = margin_columns[...]
    positions = lax.broadcasted_iota(jnp.int32, (LANES, LANES), 0)
    for slot in range(SLOTS):
        here = positions == ids[slot : slot + 1, :]
        chosen[:, slot * LANES : (slot + 1) * LANES] = here.astype(f32).astype(bf16)


def fill_gathered(vector, chosen, gathered):
    product = jnp.dot(vector, chosen[...], preferred_element_type=f32).astype(bf16)
    for slot in range(SLOTS):
        gathered[slot * BLOCK : (slot + 1) * BLOCK, :] = product[:, slot * LANES : (slot + 1) * LANES]


def own_product(rows_ref, gathered, turned):
    lanes = lane_ids()
    for start in range(0, WIDTH, LANES):
        stop = min(start + LANES, WIDTH)
        turned[:, start:stop] = gathered[start:stop, :].astype(f32).T
    total = jnp.zeros((BLOCK, LANES), f32)
    for start, stop in KTILES:
        rows = rows_ref[0:SPLIT, :, start:stop].reshape(SPLIT * BLOCK, stop - start)
        product = jnp.dot(rows, gathered[start:stop, :], preferred_element_type=f32)
        part = jnp.zeros((BLOCK, LANES), f32)
        for face in range(SPLIT):
            part = jnp.where(lanes == face, product[face * BLOCK : (face + 1) * BLOCK], part)
        total = total + part
    for face in range(SPLIT, F_DEV):
        row = turned[face : face + 1, :]
        block_row = rows_ref[face].astype(f32)
        part = jnp.zeros((BLOCK, LANES), f32)
        for start in range(0, REST, LANES):
            part = part + block_row[:, start : start + LANES] * row[:, start : start + LANES]
        value = jnp.sum(part, axis=1, keepdims=True)
        value = value + jnp.sum(block_row[:, REST:WIDTH] * row[:, REST:WIDTH], axis=1, keepdims=True)
        total = jnp.where(lanes == face, value, total)
    return total


def margin_product(messages, groups, gathered, tail):
    lanes = lane_ids()
    tail[...] = jnp.zeros(tail.shape, bf16)
    tail[0:64, 0:LANES] = gathered[256:320, :]
    tail[64:128, LANES : 2 * LANES] = gathered[256:320, :]
    total = jnp.zeros((BLOCK, LANES), f32)
    ends = jnp.zeros((BLOCK, LANES), f32)
    for message, (group, there) in zip(messages, groups):
        rows = jnp.concatenate([message[:, 0:BLOCK, :], message[:, BLOCK : 2 * BLOCK, :]], axis=-1)
        product = jnp.dot(rows.reshape(LIST * BLOCK, 256), gathered[0:256, :], preferred_element_type=f32)
        rest = message[:, 2 * BLOCK : MESSAGE, :].reshape(LIST * 48, LANES)
        second = jnp.dot(rest, tail[...], preferred_element_type=f32)
        for face in range(LIST):
            chosen = (lanes == F_DEV + group * LIST + face) & there
            total = jnp.where(chosen, product[face * BLOCK : (face + 1) * BLOCK], total)
            part = second[face * 48 : face * 48 + 40]
            ends = jnp.where(chosen, jnp.concatenate([part[:, 0:LANES], part[:, LANES:]], axis=0), ends)
    return total + ends


def pack_kernel(indices, lists, rows, basis, out0, out1, latest, wide, staged, sem_latest, sems):
    first = pltpu.make_async_copy(basis.at[KRYLOV - 1], latest, sem_latest)
    first.start()
    outs = (out0, out1)
    numbers = [sent_lists()[index] for index in indices]
    copies = []
    for place in range(2):
        for face in range(LIST):
            slot = place * LIST + face
            source = rows.at[lists[numbers[place], face], :, pl.ds(0, LEAD)]
            copies.append(pltpu.make_async_copy(source, staged.at[slot], sems.at[slot]))
            copies[-1].start()
    first.wait()
    wide[:, 0:BLOCK] = latest[...].astype(f32)
    wide[:, BLOCK:LANES] = jnp.zeros((F_DEV, LANES - BLOCK), f32)
    lanes = lax.broadcasted_iota(jnp.int32, (40, LANES), 1)
    for place, out in enumerate(outs):
        for face in range(LIST):
            copies[place * LIST + face].wait()
        for face in range(LIST):
            slot = place * LIST + face
            out[face, 0:BLOCK, :] = staged[slot, :, 0:LANES]
            out[face, BLOCK : 2 * BLOCK, :] = staged[slot, :, LANES : 2 * LANES]
            end = staged[slot, :, 2 * LANES : LEAD].astype(f32)
            both = jnp.where(lanes < 64, end[0:40], pltpu.roll(end[40:80], 64, 1))
            value = jnp.broadcast_to(wide[pl.ds(lists[numbers[place], face], 1), :], (8, LANES))
            out[face, 2 * BLOCK : MESSAGE, :] = jnp.concatenate([both, value], axis=0).astype(bf16)


def pack(indices, send_lists, blocks, basis):
    return pl.pallas_call(
        functools.partial(pack_kernel, indices),
        out_shape=[shape((LIST, MESSAGE, LANES), bf16)] * 2,
        in_specs=[SMEM, ANY, ANY],
        out_specs=[VMEM] * 2,
        scratch_shapes=[
            pltpu.VMEM((F_DEV, BLOCK), bf16),
            pltpu.VMEM((F_DEV, LANES), f32),
            pltpu.VMEM((2 * LIST, BLOCK, LEAD), bf16),
            pltpu.SemaphoreType.DMA,
            pltpu.SemaphoreType.DMA((2 * LIST,)),
        ],
        compiler_params=PACK_PARAMS,
        name="pack_span" if indices[0] > 1 else "pack_pitch",
    )(send_lists, blocks, basis)


def sweeps_kernel(
    rows, chosen, lists, basis, m3, m2, m1, m0,
    precond_out, out0, out1, out2, out3, wide, gathered, turned, tail,
):
    factors = sweep_constants()
    messages, groups = (m0, m1, m2, m3), received_groups()
    wide[...] = jnp.zeros((LANES, LANES), f32)
    wide[0:F_DEV, 0:BLOCK] = basis[KRYLOV - 1].astype(f32)
    for message, (group, there) in zip(messages, groups):
        start = pl.multiple_of(F_DEV + group * LIST, LIST)
        last = [message[face, MESSAGE - 16 : MESSAGE, :].astype(f32)[8:9] for face in range(LIST)]
        wide[pl.ds(start, LIST), :] = jnp.where(there, jnp.concatenate(last, axis=0), 0.0)
    residual = wide[...].T[0:BLOCK]
    direction = residual / center_value
    solution = direction
    for sweep in range(SWEEPS - 1):
        fill_gathered(direction.astype(bf16), chosen, gathered)
        applied = own_product(rows, gathered, turned)
        if sweep < SWEEPS - 2:
            applied = applied + margin_product(messages, groups, gathered, tail)
        residual = residual - applied
        keep_factor, push_factor = factors[sweep]
        direction = keep_factor * direction + push_factor * residual
        solution = solution + direction
    own = jnp.where(lane_ids() < F_DEV, solution, 0.0).astype(bf16)
    precond_out[...] = own
    wide[0:BLOCK, :] = own.astype(f32)
    wide[BLOCK:LANES, :] = jnp.zeros((LANES - BLOCK, LANES), f32)
    wide[...] = wide[...].T
    for out, number in zip((out0, out1, out2, out3), sent_lists()):
        for face in range(LIST):
            out[face : face + 1, :] = wide[pl.ds(lists[number, face], 1), :]


def image_kernel(
    rows, chosen, precond, g3, g2, g1, g0, basis, image_out, sums_out, wide, gathered, turned, sums
):
    wide[...] = jnp.zeros((LANES, LANES), f32)
    for ghost, (group, there) in zip((g0, g1, g2, g3), received_groups()):
        wide[pl.ds(pl.multiple_of(F_DEV + group * LIST, LIST), LIST), :] = jnp.where(there, ghost[...], 0.0)
    vector = precond[...] + wide[...].T[0:BLOCK].astype(bf16)
    fill_gathered(vector, chosen, gathered)
    sums[...] = jnp.zeros((LANES, LANES), f32)
    spread = [basis[j].astype(f32) for j in range(KRYLOV)]
    for a in range(KRYLOV):
        for b in range(a, KRYLOV):
            entry = jnp.sum(spread[a] * spread[b], axis=0, keepdims=True)
            for row in {GRAM + KRYLOV * a + b, GRAM + KRYLOV * b + a}:
                sums[row : row + 1, 0:BLOCK] = entry
    product = own_product(rows, gathered, turned)
    wide[0:BLOCK, :] = product
    wide[BLOCK:LANES, :] = jnp.zeros((LANES - BLOCK, LANES), f32)
    image = wide[...].T[0:F_DEV, 0:BLOCK]
    image_out[...] = image
    for j in range(KRYLOV):
        sums[j : j + 1, 0:BLOCK] = jnp.sum(spread[j] * image, axis=0, keepdims=True)
    sums[KRYLOV : KRYLOV + 1, 0:BLOCK] = jnp.sum(image * image, axis=0, keepdims=True)
    totals = jnp.sum(sums[...], axis=1, keepdims=True)
    row = jnp.broadcast_to(totals, (LANES, LANES)).T[0:1]
    sums_out[...] = jnp.broadcast_to(row, sums_out.shape)


def last_kernel(inverse_count, image, basis, sums, vector_out, projections_out, remainder_out, flag_out):
    totals = jnp.sum(sums[...], axis=0, keepdims=True) * inverse_count
    lanes = lax.broadcasted_iota(jnp.int32, (KRYLOV, LANES), 1)
    rows = lax.broadcasted_iota(jnp.int32, (KRYLOV, LANES), 0)
    heights = jnp.broadcast_to(totals, (LANES, LANES)).T[0:KRYLOV]
    left = jnp.sum(jnp.where(lanes // KRYLOV - GRAM // KRYLOV == rows, heights, 0.0), axis=0, keepdims=True)
    right = jnp.sum(jnp.where(lanes % KRYLOV == rows, heights, 0.0), axis=0, keepdims=True)
    lane = lanes[0:1]
    terms = jnp.where(lane < KRYLOV, -2.0 * totals * totals, jnp.where(lane == KRYLOV, totals, left * right * totals))
    total = totals[:, KRYLOV : KRYLOV + 1]
    squares = jnp.sum(terms, axis=1, keepdims=True)
    length = jnp.sqrt(jnp.maximum(squares, 0.0) + epsilon)
    remainder = image[...]
    for j in range(KRYLOV):
        remainder = remainder - heights[j : j + 1, 0:BLOCK] * basis[j].astype(f32)
    remainder_out[...] = remainder
    vector_out[...] = (remainder / length).astype(bf16)
    projections_out[...] = jnp.where(lane == KRYLOV, length, totals)[0, 0 : KRYLOV + 1]
    flag_out[0] = jnp.where(squares < GUARD * total, 1, 0)[0, 0]


def shape(dims, dtype):
    return jax.ShapeDtypeStruct(dims, dtype)


def per_device(blocks, columns, margin_columns, send_lists, basis):
    devices = lax.axis_size("pitch") * lax.axis_size("span")
    square = pltpu.VMEM((LANES, LANES), f32)
    gathered = pltpu.VMEM((WIDTH, LANES), bf16)
    turned = pltpu.VMEM((LANES, WIDTH), f32)

    last, third = pack((3, 2), send_lists, blocks, basis)
    second, first = pack((1, 0), send_lists, blocks, basis)
    messages = exchange([first, second, third, last])
    chosen = pl.pallas_call(
        choose_kernel,
        out_shape=shape((LANES, SLOTS * LANES), bf16),
        in_specs=[VMEM] * 3,
        out_specs=VMEM,
        scratch_shapes=[pltpu.VMEM((16, LANES), jnp.int32)],
        compiler_params=PARAMS,
        cost_estimate=pl.CostEstimate(flops=0, bytes_accessed=2**20, transcendentals=0),
        name="choose",
    )(blocks, columns.T, margin_columns.T)
    precond, *values = pl.pallas_call(
        sweeps_kernel,
        out_shape=[shape((BLOCK, LANES), bf16)] + [shape((LIST, LANES), f32)] * 4,
        in_specs=[VMEM, VMEM, SMEM] + [VMEM] * 5,
        out_specs=[VMEM] * 5,
        scratch_shapes=[square, gathered, turned, pltpu.VMEM((LANES, 2 * LANES), bf16)],
        compiler_params=PARAMS,
        name="sweeps",
    )(blocks, chosen, send_lists, basis, *messages[::-1])
    ghosts = exchange(values)
    image, sums = pl.pallas_call(
        image_kernel,
        out_shape=[shape((F_DEV, BLOCK), f32), shape((devices, LANES), f32)],
        in_specs=[VMEM] * 8,
        out_specs=[VMEM] * 2,
        scratch_shapes=[square, gathered, turned, square],
        compiler_params=PARAMS,
        name="image",
    )(blocks, chosen, precond, *ghosts[::-1], basis)
    sums = lax.all_to_all(sums.reshape(devices, 1, LANES), ("pitch", "span"), 0, 0)
    inverse_count = 1.0 / (devices * F_DEV * BLOCK)
    new_vector, projections, remainder, cancelled = pl.pallas_call(
        functools.partial(last_kernel, inverse_count),
        out_shape=[
            shape((F_DEV, BLOCK), bf16),
            shape((KRYLOV + 1,), f32),
            shape((F_DEV, BLOCK), f32),
            shape((1,), jnp.int32),
        ],
        in_specs=[VMEM] * 3,
        out_specs=[VMEM] * 3 + [SMEM],
        name="new_vector",
    )(image, basis, sums.reshape(devices, LANES))

    def summed_again(state):
        squares = lax.psum(jnp.sum(remainder * remainder), ("pitch", "span")) * inverse_count
        length = jnp.sqrt(squares + epsilon)
        return jnp.zeros_like(state[0]), (remainder / length).astype(bf16), state[2].at[KRYLOV].set(length)

    state = (cancelled, new_vector, projections)
    return lax.while_loop(lambda state: state[0][0] == 1, summed_again, state)[1:]


def solution(mesh):
    return jax.shard_map(
        per_device,
        mesh=mesh,
        in_specs=(
            P(("pitch", "span"), None, None),
            P(("pitch", "span"), None),
            P(("pitch", "span"), None),
            P(("pitch", "span"), None),
            P(None, ("pitch", "span"), None),
        ),
        out_specs=(P(("pitch", "span"), None), P()),
        check_vma=False,
    )
```

```python
import functools

import jax
import jax.numpy as jnp
from jax import lax
from jax.experimental import pallas as pl
from jax.experimental.pallas import tpu as pltpu
from jax.sharding import PartitionSpec as P

BLOCK = 80
SLOTS = 11
GSLOTS = 4
F_DEV = 64
KRYLOV = 8
SWEEPS = 4
LIST = 8
LANES = 128
WIDTH = SLOTS * BLOCK
LEAD = 384
MESSAGE = 208
GRAM = 64
GUARD = 2.0**-11
KTILES = ((0, 256), (256, 512), (512, 768), (768, 880))
REST = 768
SPLIT = 24

center_value = 1.0
half_width = 0.5
epsilon = 1e-06

f32 = jnp.float32
bf16 = jnp.bfloat16
VMEM = pl.BlockSpec(memory_space=pltpu.VMEM)
SMEM = pl.BlockSpec(memory_space=pltpu.SMEM)
ANY = pl.BlockSpec(memory_space=pl.ANY)
PARAMS = pltpu.CompilerParams(vmem_limit_bytes=32 * 2**20)
PACK_PARAMS = pltpu.CompilerParams(vmem_limit_bytes=58 * 2**20)


def sweep_constants():
    stretch = center_value / half_width
    ratio_now = 1.0 / stretch
    factors = []
    for _ in range(SWEEPS - 1):
        ratio_next = 1.0 / (2.0 * stretch - ratio_now)
        factors.append((ratio_next * ratio_now, 2.0 * ratio_next / half_width))
        ratio_now = ratio_next
    return factors


def positions():
    return lax.axis_index("pitch") % 2, lax.axis_index("span") % 2


def sent_lists():
    pitch_odd, span_odd = positions()
    return pitch_odd, 1 - pitch_odd, 2 + span_odd, 3 - span_odd


def received_groups():
    pitch_odd, span_odd = positions()
    span = lax.axis_index("span")
    inside = (span != 0) & (span != lax.axis_size("span") - 1)
    return (1 - pitch_odd, True), (pitch_odd, True), (3 - span_odd, True), (2 + span_odd, inside)


def exchange(outgoing):
    received = [None] * 4
    for index in (3, 2, 1, 0):
        axis = "pitch" if index < 2 else "span"
        devices = lax.axis_size(axis)
        pairs = []
        for low in range(index % 2, devices, 2):
            high = (low + 1) % devices
            pairs += [(low, high), (high, low)]
        received[index] = lax.ppermute(outgoing[index], axis, pairs)
    return received


def lane_ids():
    return lax.broadcasted_iota(jnp.int32, (BLOCK, LANES), 1)


def choose_kernel(rows, columns, margin_columns, basis, chosen, gram, ids):
    gram[...] = jnp.zeros(gram.shape, f32)
    vectors = [basis[j].astype(f32) for j in range(KRYLOV)]
    for a in range(KRYLOV):
        for b in range(a, KRYLOV):
            entry = jnp.sum(vectors[a] * vectors[b], axis=0, keepdims=True)
            for row in {KRYLOV * a + b, KRYLOV * b + a}:
                gram[row : row + 1, 0:BLOCK] = entry
    ids[...] = jnp.full(ids.shape, LANES - 1, jnp.int32)
    ids[0:SLOTS, 0:F_DEV] = columns[...]
    ids[0:GSLOTS, F_DEV : F_DEV + 4 * LIST] = margin_columns[...]
    positions = lax.broadcasted_iota(jnp.int32, (LANES, LANES), 0)
    for slot in range(SLOTS):
        here = positions == ids[slot : slot + 1, :]
        chosen[:, slot * LANES : (slot + 1) * LANES] = here.astype(f32).astype(bf16)


def fill_gathered(vector, chosen, gathered):
    product = jnp.dot(vector, chosen[...], preferred_element_type=f32).astype(bf16)
    for slot in range(SLOTS):
        gathered[slot * BLOCK : (slot + 1) * BLOCK, :] = product[:, slot * LANES : (slot + 1) * LANES]


def own_product(rows_ref, gathered, turned):
    lanes = lane_ids()
    for start in range(0, WIDTH, LANES):
        stop = min(start + LANES, WIDTH)
        turned[:, start:stop] = gathered[start:stop, :].astype(f32).T
    total = jnp.zeros((BLOCK, LANES), f32)
    for start, stop in KTILES:
        rows = rows_ref[0:SPLIT, :, start:stop].reshape(SPLIT * BLOCK, stop - start)
        product = jnp.dot(rows, gathered[start:stop, :], preferred_element_type=f32)
        part = jnp.zeros((BLOCK, LANES), f32)
        for face in range(SPLIT):
            part = jnp.where(lanes == face, product[face * BLOCK : (face + 1) * BLOCK], part)
        total = total + part
    for face in range(SPLIT, F_DEV):
        row = turned[face : face + 1, :]
        block_row = rows_ref[face].astype(f32)
        part = jnp.zeros((BLOCK, LANES), f32)
        for start in range(0, REST, LANES):
            part = part + block_row[:, start : start + LANES] * row[:, start : start + LANES]
        value = jnp.sum(part, axis=1, keepdims=True)
        value = value + jnp.sum(block_row[:, REST:WIDTH] * row[:, REST:WIDTH], axis=1, keepdims=True)
        total = jnp.where(lanes == face, value, total)
    return total


def margin_product(messages, groups, gathered, tail):
    lanes = lane_ids()
    tail[...] = jnp.zeros(tail.shape, bf16)
    tail[0:64, 0:LANES] = gathered[256:320, :]
    tail[64:128, LANES : 2 * LANES] = gathered[256:320, :]
    total = jnp.zeros((BLOCK, LANES), f32)
    ends = jnp.zeros((BLOCK, LANES), f32)
    for message, (group, there) in zip(messages, groups):
        rows = jnp.concatenate([message[:, 0:BLOCK, :], message[:, BLOCK : 2 * BLOCK, :]], axis=-1)
        product = jnp.dot(rows.reshape(LIST * BLOCK, 256), gathered[0:256, :], preferred_element_type=f32)
        rest = message[:, 2 * BLOCK : MESSAGE, :].reshape(LIST * 48, LANES)
        second = jnp.dot(rest, tail[...], preferred_element_type=f32)
        for face in range(LIST):
            chosen = (lanes == F_DEV + group * LIST + face) & there
            total = jnp.where(chosen, product[face * BLOCK : (face + 1) * BLOCK], total)
            part = second[face * 48 : face * 48 + 40]
            ends = jnp.where(chosen, jnp.concatenate([part[:, 0:LANES], part[:, LANES:]], axis=0), ends)
    return total + ends


def pack_kernel(indices, lists, rows, basis, out0, out1, latest, wide, staged, sem_latest, sems):
    first = pltpu.make_async_copy(basis.at[KRYLOV - 1], latest, sem_latest)
    first.start()
    outs = (out0, out1)
    numbers = [sent_lists()[index] for index in indices]
    copies = []
    for place in range(2):
        for face in range(LIST):
            slot = place * LIST + face
            source = rows.at[lists[numbers[place], face], :, pl.ds(0, LEAD)]
            copies.append(pltpu.make_async_copy(source, staged.at[slot], sems.at[slot]))
            copies[-1].start()
    first.wait()
    wide[:, 0:BLOCK] = latest[...].astype(f32)
    wide[:, BLOCK:LANES] = jnp.zeros((F_DEV, LANES - BLOCK), f32)
    lanes = lax.broadcasted_iota(jnp.int32, (40, LANES), 1)
    for place, out in enumerate(outs):
        for face in range(LIST):
            copies[place * LIST + face].wait()
        for face in range(LIST):
            slot = place * LIST + face
            out[face, 0:BLOCK, :] = staged[slot, :, 0:LANES]
            out[face, BLOCK : 2 * BLOCK, :] = staged[slot, :, LANES : 2 * LANES]
            end = staged[slot, :, 2 * LANES : LEAD].astype(f32)
            both = jnp.where(lanes < 64, end[0:40], pltpu.roll(end[40:80], 64, 1))
            value = jnp.broadcast_to(wide[pl.ds(lists[numbers[place], face], 1), :], (8, LANES))
            out[face, 2 * BLOCK : MESSAGE, :] = jnp.concatenate([both, value], axis=0).astype(bf16)


def pack(indices, send_lists, blocks, basis):
    return pl.pallas_call(
        functools.partial(pack_kernel, indices),
        out_shape=[shape((LIST, MESSAGE, LANES), bf16)] * 2,
        in_specs=[SMEM, ANY, ANY],
        out_specs=[VMEM] * 2,
        scratch_shapes=[
            pltpu.VMEM((F_DEV, BLOCK), bf16),
            pltpu.VMEM((F_DEV, LANES), f32),
            pltpu.VMEM((2 * LIST, BLOCK, LEAD), bf16),
            pltpu.SemaphoreType.DMA,
            pltpu.SemaphoreType.DMA((2 * LIST,)),
        ],
        compiler_params=PACK_PARAMS,
        name="pack_span" if indices[0] > 1 else "pack_pitch",
    )(send_lists, blocks, basis)


def sweeps_kernel(
    rows, chosen, lists, basis, m3, m2, m1, m0,
    precond_out, out0, out1, out2, out3, wide, gathered, turned, tail,
):
    factors = sweep_constants()
    messages, groups = (m0, m1, m2, m3), received_groups()
    wide[...] = jnp.zeros((LANES, LANES), f32)
    wide[0:F_DEV, 0:BLOCK] = basis[KRYLOV - 1].astype(f32)
    for message, (group, there) in zip(messages, groups):
        start = pl.multiple_of(F_DEV + group * LIST, LIST)
        last = [message[face, MESSAGE - 16 : MESSAGE, :].astype(f32)[8:9] for face in range(LIST)]
        wide[pl.ds(start, LIST), :] = jnp.where(there, jnp.concatenate(last, axis=0), 0.0)
    residual = wide[...].T[0:BLOCK]
    direction = residual / center_value
    solution = direction
    for sweep in range(SWEEPS - 1):
        fill_gathered(direction.astype(bf16), chosen, gathered)
        applied = own_product(rows, gathered, turned)
        if sweep < SWEEPS - 2:
            applied = applied + margin_product(messages, groups, gathered, tail)
        residual = residual - applied
        keep_factor, push_factor = factors[sweep]
        direction = keep_factor * direction + push_factor * residual
        solution = solution + direction
    own = jnp.where(lane_ids() < F_DEV, solution, 0.0).astype(bf16)
    precond_out[...] = own
    wide[0:BLOCK, :] = own.astype(f32)
    wide[BLOCK:LANES, :] = jnp.zeros((LANES - BLOCK, LANES), f32)
    wide[...] = wide[...].T
    for out, number in zip((out0, out1, out2, out3), sent_lists()):
        for face in range(LIST):
            out[face : face + 1, :] = wide[pl.ds(lists[number, face], 1), :]


def image_kernel(
    rows, chosen, precond, g0, g1, g2, g3, basis, gram, image_out, sums_out, wide, gathered, turned, sums
):
    wide[...] = jnp.zeros((LANES, LANES), f32)
    for ghost, (group, there) in zip((g0, g1, g2, g3), received_groups()):
        wide[pl.ds(pl.multiple_of(F_DEV + group * LIST, LIST), LIST), :] = jnp.where(there, ghost[...], 0.0)
    vector = precond[...] + wide[...].T[0:BLOCK].astype(bf16)
    fill_gathered(vector, chosen, gathered)
    sums[0:GRAM, :] = jnp.zeros((GRAM, LANES), f32)
    sums[GRAM:LANES, :] = gram[...]
    product = own_product(rows, gathered, turned)
    wide[0:BLOCK, :] = product
    wide[BLOCK:LANES, :] = jnp.zeros((LANES - BLOCK, LANES), f32)
    image = wide[...].T[0:F_DEV, 0:BLOCK]
    image_out[...] = image
    for j in range(KRYLOV):
        sums[j : j + 1, 0:BLOCK] = jnp.sum(basis[j].astype(f32) * image, axis=0, keepdims=True)
    sums[KRYLOV : KRYLOV + 1, 0:BLOCK] = jnp.sum(image * image, axis=0, keepdims=True)
    totals = jnp.sum(sums[...], axis=1, keepdims=True)
    row = jnp.broadcast_to(totals, (LANES, LANES)).T[0:1]
    sums_out[...] = jnp.broadcast_to(row, sums_out.shape)


def last_kernel(inverse_count, image, basis, sums, vector_out, projections_out, remainder_out, flag_out):
    totals = jnp.sum(sums[...], axis=0, keepdims=True) * inverse_count
    lanes = lax.broadcasted_iota(jnp.int32, (KRYLOV, LANES), 1)
    rows = lax.broadcasted_iota(jnp.int32, (KRYLOV, LANES), 0)
    heights = jnp.broadcast_to(totals, (LANES, LANES)).T[0:KRYLOV]
    left = jnp.sum(jnp.where(lanes // KRYLOV - GRAM // KRYLOV == rows, heights, 0.0), axis=0, keepdims=True)
    right = jnp.sum(jnp.where(lanes % KRYLOV == rows, heights, 0.0), axis=0, keepdims=True)
    lane = lanes[0:1]
    terms = jnp.where(lane < KRYLOV, -2.0 * totals * totals, jnp.where(lane == KRYLOV, totals, left * right * totals))
    total = totals[:, KRYLOV : KRYLOV + 1]
    squares = jnp.sum(terms, axis=1, keepdims=True)
    length = jnp.sqrt(jnp.maximum(squares, 0.0) + epsilon)
    remainder = image[...]
    for j in range(KRYLOV):
        remainder = remainder - heights[j : j + 1, 0:BLOCK] * basis[j].astype(f32)
    remainder_out[...] = remainder
    vector_out[...] = (remainder / length).astype(bf16)
    projections_out[...] = jnp.where(lane == KRYLOV, length, totals)[0, 0 : KRYLOV + 1]
    flag_out[0] = jnp.where(squares < GUARD * total, 1, 0)[0, 0]


def shape(dims, dtype):
    return jax.ShapeDtypeStruct(dims, dtype)


def per_device(blocks, columns, margin_columns, send_lists, basis):
    devices = lax.axis_size("pitch") * lax.axis_size("span")
    square = pltpu.VMEM((LANES, LANES), f32)
    gathered = pltpu.VMEM((WIDTH, LANES), bf16)
    turned = pltpu.VMEM((LANES, WIDTH), f32)

    last, third = pack((3, 2), send_lists, blocks, basis)
    second, first = pack((1, 0), send_lists, blocks, basis)
    messages = exchange([first, second, third, last])
    chosen, gram = pl.pallas_call(
        choose_kernel,
        out_shape=[shape((LANES, SLOTS * LANES), bf16), shape((LANES - GRAM, LANES), f32)],
        in_specs=[VMEM] * 4,
        out_specs=[VMEM] * 2,
        scratch_shapes=[pltpu.VMEM((16, LANES), jnp.int32)],
        compiler_params=PARAMS,
        cost_estimate=pl.CostEstimate(flops=0, bytes_accessed=2**20, transcendentals=0),
        name="choose",
    )(blocks, columns.T, margin_columns.T, basis)
    precond, *values = pl.pallas_call(
        sweeps_kernel,
        out_shape=[shape((BLOCK, LANES), bf16)] + [shape((LIST, LANES), f32)] * 4,
        in_specs=[VMEM, VMEM, SMEM] + [VMEM] * 5,
        out_specs=[VMEM] * 5,
        scratch_shapes=[square, gathered, turned, pltpu.VMEM((LANES, 2 * LANES), bf16)],
        compiler_params=PARAMS,
        name="sweeps",
    )(blocks, chosen, send_lists, basis, *messages[::-1])
    ghosts = exchange(values)
    image, sums = pl.pallas_call(
        image_kernel,
        out_shape=[shape((F_DEV, BLOCK), f32), shape((devices, LANES), f32)],
        in_specs=[VMEM] * 9,
        out_specs=[VMEM] * 2,
        scratch_shapes=[square, gathered, turned, square],
        compiler_params=PARAMS,
        name="image",
    )(blocks, chosen, precond, *ghosts, basis, gram)
    sums = lax.all_to_all(sums.reshape(devices, 1, LANES), ("pitch", "span"), 0, 0)
    inverse_count = 1.0 / (devices * F_DEV * BLOCK)
    new_vector, projections, remainder, cancelled = pl.pallas_call(
        functools.partial(last_kernel, inverse_count),
        out_shape=[
            shape((F_DEV, BLOCK), bf16),
            shape((KRYLOV + 1,), f32),
            shape((F_DEV, BLOCK), f32),
            shape((1,), jnp.int32),
        ],
        in_specs=[VMEM] * 3,
        out_specs=[VMEM] * 3 + [SMEM],
        name="new_vector",
    )(image, basis, sums.reshape(devices, LANES))

    def summed_again(state):
        squares = lax.psum(jnp.sum(remainder * remainder), ("pitch", "span")) * inverse_count
        length = jnp.sqrt(squares + epsilon)
        return jnp.zeros_like(state[0]), (remainder / length).astype(bf16), state[2].at[KRYLOV].set(length)

    state = (cancelled, new_vector, projections)
    return lax.while_loop(lambda state: state[0][0] == 1, summed_again, state)[1:]


def solution(mesh):
    return jax.shard_map(
        per_device,
        mesh=mesh,
        in_specs=(
            P(("pitch", "span"), None, None),
            P(("pitch", "span"), None),
            P(("pitch", "span"), None),
            P(("pitch", "span"), None),
            P(None, ("pitch", "span"), None),
        ),
        out_specs=(P(("pitch", "span"), None), P()),
        check_vma=False,
    )
```

```python
import functools

import jax
import jax.numpy as jnp
from jax import lax
from jax.experimental import pallas as pl
from jax.experimental.pallas import tpu as pltpu
from jax.sharding import PartitionSpec as P

BLOCK = 80
SLOTS = 11
GSLOTS = 4
F_DEV = 64
KRYLOV = 8
SWEEPS = 4
LIST = 8
LANES = 128
WIDTH = SLOTS * BLOCK
LEAD = 384
MESSAGE = 208
GRAM = 64
GUARD = 2.0**-11
KTILES = ((0, 256), (256, 512), (512, 768), (768, 880))
REST = 768
SPLIT = 22

center_value = 1.0
half_width = 0.5
epsilon = 1e-06

f32 = jnp.float32
bf16 = jnp.bfloat16
VMEM = pl.BlockSpec(memory_space=pltpu.VMEM)
SMEM = pl.BlockSpec(memory_space=pltpu.SMEM)
ANY = pl.BlockSpec(memory_space=pl.ANY)
PARAMS = pltpu.CompilerParams(vmem_limit_bytes=32 * 2**20)
PACK_PARAMS = pltpu.CompilerParams(vmem_limit_bytes=58 * 2**20)


def sweep_constants():
    stretch = center_value / half_width
    ratio_now = 1.0 / stretch
    factors = []
    for _ in range(SWEEPS - 1):
        ratio_next = 1.0 / (2.0 * stretch - ratio_now)
        factors.append((ratio_next * ratio_now, 2.0 * ratio_next / half_width))
        ratio_now = ratio_next
    return factors


def positions():
    return lax.axis_index("pitch") % 2, lax.axis_index("span") % 2


def sent_lists():
    pitch_odd, span_odd = positions()
    return pitch_odd, 1 - pitch_odd, 2 + span_odd, 3 - span_odd


def received_groups():
    pitch_odd, span_odd = positions()
    span = lax.axis_index("span")
    inside = (span != 0) & (span != lax.axis_size("span") - 1)
    return (1 - pitch_odd, True), (pitch_odd, True), (3 - span_odd, True), (2 + span_odd, inside)


def exchange(outgoing):
    received = [None] * 4
    for index in (3, 2, 1, 0):
        axis = "pitch" if index < 2 else "span"
        devices = lax.axis_size(axis)
        pairs = []
        for low in range(index % 2, devices, 2):
            high = (low + 1) % devices
            pairs += [(low, high), (high, low)]
        received[index] = lax.ppermute(outgoing[index], axis, pairs)
    return received


def lane_ids():
    return lax.broadcasted_iota(jnp.int32, (BLOCK, LANES), 1)


def choose_kernel(rows, columns, margin_columns, basis, chosen, gram, ids):
    gram[...] = jnp.zeros(gram.shape, f32)
    vectors = [basis[j].astype(f32) for j in range(KRYLOV)]
    for a in range(KRYLOV):
        for b in range(a, KRYLOV):
            entry = jnp.sum(vectors[a] * vectors[b], axis=0, keepdims=True)
            for row in {KRYLOV * a + b, KRYLOV * b + a}:
                gram[row : row + 1, 0:BLOCK] = entry
    ids[...] = jnp.full(ids.shape, LANES - 1, jnp.int32)
    ids[0:SLOTS, 0:F_DEV] = columns[...]
    ids[0:GSLOTS, F_DEV : F_DEV + 4 * LIST] = margin_columns[...]
    positions = lax.broadcasted_iota(jnp.int32, (LANES, LANES), 0)
    for slot in range(SLOTS):
        here = positions == ids[slot : slot + 1, :]
        chosen[:, slot * LANES : (slot + 1) * LANES] = here.astype(f32).astype(bf16)


def fill_gathered(vector, chosen, gathered):
    product = jnp.dot(vector, chosen[...], preferred_element_type=f32).astype(bf16)
    for slot in range(SLOTS):
        gathered[slot * BLOCK : (slot + 1) * BLOCK, :] = product[:, slot * LANES : (slot + 1) * LANES]


def own_product(rows_ref, gathered, turned):
    lanes = lane_ids()
    for start in range(0, WIDTH, LANES):
        stop = min(start + LANES, WIDTH)
        turned[:, start:stop] = gathered[start:stop, :].astype(f32).T
    total = jnp.zeros((BLOCK, LANES), f32)
    for start, stop in KTILES:
        rows = rows_ref[0:SPLIT, :, start:stop].reshape(SPLIT * BLOCK, stop - start)
        product = jnp.dot(rows, gathered[start:stop, :], preferred_element_type=f32)
        part = jnp.zeros((BLOCK, LANES), f32)
        for face in range(SPLIT):
            part = jnp.where(lanes == face, product[face * BLOCK : (face + 1) * BLOCK], part)
        total = total + part
    for face in range(SPLIT, F_DEV):
        row = turned[face : face + 1, :]
        block_row = rows_ref[face].astype(f32)
        part = jnp.zeros((BLOCK, LANES), f32)
        for start in range(0, REST, LANES):
            part = part + block_row[:, start : start + LANES] * row[:, start : start + LANES]
        value = jnp.sum(part, axis=1, keepdims=True)
        value = value + jnp.sum(block_row[:, REST:WIDTH] * row[:, REST:WIDTH], axis=1, keepdims=True)
        total = jnp.where(lanes == face, value, total)
    return total


def margin_product(messages, groups, gathered, tail):
    lanes = lane_ids()
    tail[...] = jnp.zeros(tail.shape, bf16)
    tail[0:64, 0:LANES] = gathered[256:320, :]
    tail[64:128, LANES : 2 * LANES] = gathered[256:320, :]
    total = jnp.zeros((BLOCK, LANES), f32)
    ends = jnp.zeros((BLOCK, LANES), f32)
    for message, (group, there) in zip(messages, groups):
        rows = jnp.concatenate([message[:, 0:BLOCK, :], message[:, BLOCK : 2 * BLOCK, :]], axis=-1)
        product = jnp.dot(rows.reshape(LIST * BLOCK, 256), gathered[0:256, :], preferred_element_type=f32)
        rest = message[:, 2 * BLOCK : MESSAGE, :].reshape(LIST * 48, LANES)
        second = jnp.dot(rest, tail[...], preferred_element_type=f32)
        for face in range(LIST):
            chosen = (lanes == F_DEV + group * LIST + face) & there
            total = jnp.where(chosen, product[face * BLOCK : (face + 1) * BLOCK], total)
            part = second[face * 48 : face * 48 + 40]
            ends = jnp.where(chosen, jnp.concatenate([part[:, 0:LANES], part[:, LANES:]], axis=0), ends)
    return total + ends


def pack_kernel(indices, lists, rows, basis, out0, out1, latest, wide, staged, sem_latest, sems):
    first = pltpu.make_async_copy(basis.at[KRYLOV - 1], latest, sem_latest)
    first.start()
    outs = (out0, out1)
    numbers = [sent_lists()[index] for index in indices]
    copies = []
    for place in range(2):
        for face in range(LIST):
            slot = place * LIST + face
            source = rows.at[lists[numbers[place], face], :, pl.ds(0, LEAD)]
            copies.append(pltpu.make_async_copy(source, staged.at[slot], sems.at[slot]))
            copies[-1].start()
    first.wait()
    wide[:, 0:BLOCK] = latest[...].astype(f32)
    wide[:, BLOCK:LANES] = jnp.zeros((F_DEV, LANES - BLOCK), f32)
    lanes = lax.broadcasted_iota(jnp.int32, (40, LANES), 1)
    for place, out in enumerate(outs):
        for face in range(LIST):
            copies[place * LIST + face].wait()
        for face in range(LIST):
            slot = place * LIST + face
            out[face, 0:BLOCK, :] = staged[slot, :, 0:LANES]
            out[face, BLOCK : 2 * BLOCK, :] = staged[slot, :, LANES : 2 * LANES]
            end = staged[slot, :, 2 * LANES : LEAD].astype(f32)
            both = jnp.where(lanes < 64, end[0:40], pltpu.roll(end[40:80], 64, 1))
            value = jnp.broadcast_to(wide[pl.ds(lists[numbers[place], face], 1), :], (8, LANES))
            out[face, 2 * BLOCK : MESSAGE, :] = jnp.concatenate([both, value], axis=0).astype(bf16)


def pack(indices, send_lists, blocks, basis):
    return pl.pallas_call(
        functools.partial(pack_kernel, indices),
        out_shape=[shape((LIST, MESSAGE, LANES), bf16)] * 2,
        in_specs=[SMEM, ANY, ANY],
        out_specs=[VMEM] * 2,
        scratch_shapes=[
            pltpu.VMEM((F_DEV, BLOCK), bf16),
            pltpu.VMEM((F_DEV, LANES), f32),
            pltpu.VMEM((2 * LIST, BLOCK, LEAD), bf16),
            pltpu.SemaphoreType.DMA,
            pltpu.SemaphoreType.DMA((2 * LIST,)),
        ],
        compiler_params=PACK_PARAMS,
        name="pack_span" if indices[0] > 1 else "pack_pitch",
    )(send_lists, blocks, basis)


def sweeps_kernel(
    rows, chosen, lists, basis, m3, m2, m1, m0,
    precond_out, out0, out1, out2, out3, wide, gathered, turned, tail,
):
    factors = sweep_constants()
    messages, groups = (m0, m1, m2, m3), received_groups()
    wide[...] = jnp.zeros((LANES, LANES), f32)
    wide[0:F_DEV, 0:BLOCK] = basis[KRYLOV - 1].astype(f32)
    for message, (group, there) in zip(messages, groups):
        start = pl.multiple_of(F_DEV + group * LIST, LIST)
        last = [message[face, MESSAGE - 16 : MESSAGE, :].astype(f32)[8:9] for face in range(LIST)]
        wide[pl.ds(start, LIST), :] = jnp.where(there, jnp.concatenate(last, axis=0), 0.0)
    residual = wide[...].T[0:BLOCK]
    direction = residual / center_value
    solution = direction
    for sweep in range(SWEEPS - 1):
        fill_gathered(direction.astype(bf16), chosen, gathered)
        applied = own_product(rows, gathered, turned)
        if sweep < SWEEPS - 2:
            applied = applied + margin_product(messages, groups, gathered, tail)
        residual = residual - applied
        keep_factor, push_factor = factors[sweep]
        direction = keep_factor * direction + push_factor * residual
        solution = solution + direction
    own = jnp.where(lane_ids() < F_DEV, solution, 0.0).astype(bf16)
    precond_out[...] = own
    wide[0:BLOCK, :] = own.astype(f32)
    wide[BLOCK:LANES, :] = jnp.zeros((LANES - BLOCK, LANES), f32)
    wide[...] = wide[...].T
    for out, number in zip((out0, out1, out2, out3), sent_lists()):
        for face in range(LIST):
            out[face : face + 1, :] = wide[pl.ds(lists[number, face], 1), :]


def image_kernel(
    rows, chosen, precond, g0, g1, g2, g3, basis, gram, image_out, sums_out, wide, gathered, turned, sums
):
    wide[...] = jnp.zeros((LANES, LANES), f32)
    for ghost, (group, there) in zip((g0, g1, g2, g3), received_groups()):
        wide[pl.ds(pl.multiple_of(F_DEV + group * LIST, LIST), LIST), :] = jnp.where(there, ghost[...], 0.0)
    vector = precond[...] + wide[...].T[0:BLOCK].astype(bf16)
    fill_gathered(vector, chosen, gathered)
    sums[0:GRAM, :] = jnp.zeros((GRAM, LANES), f32)
    sums[GRAM:LANES, :] = gram[...]
    product = own_product(rows, gathered, turned)
    wide[0:BLOCK, :] = product
    wide[BLOCK:LANES, :] = jnp.zeros((LANES - BLOCK, LANES), f32)
    image = wide[...].T[0:F_DEV, 0:BLOCK]
    image_out[...] = image
    for j in range(KRYLOV):
        sums[j : j + 1, 0:BLOCK] = jnp.sum(basis[j].astype(f32) * image, axis=0, keepdims=True)
    sums[KRYLOV : KRYLOV + 1, 0:BLOCK] = jnp.sum(image * image, axis=0, keepdims=True)
    totals = jnp.sum(sums[...], axis=1, keepdims=True)
    row = jnp.broadcast_to(totals, (LANES, LANES)).T[0:1]
    sums_out[...] = jnp.broadcast_to(row, sums_out.shape)


def last_kernel(inverse_count, image, basis, sums, vector_out, projections_out, remainder_out, flag_out):
    totals = jnp.sum(sums[...], axis=0, keepdims=True) * inverse_count
    lanes = lax.broadcasted_iota(jnp.int32, (KRYLOV, LANES), 1)
    rows = lax.broadcasted_iota(jnp.int32, (KRYLOV, LANES), 0)
    heights = jnp.broadcast_to(totals, (LANES, LANES)).T[0:KRYLOV]
    left = jnp.sum(jnp.where(lanes // KRYLOV - GRAM // KRYLOV == rows, heights, 0.0), axis=0, keepdims=True)
    right = jnp.sum(jnp.where(lanes % KRYLOV == rows, heights, 0.0), axis=0, keepdims=True)
    lane = lanes[0:1]
    terms = jnp.where(lane < KRYLOV, -2.0 * totals * totals, jnp.where(lane == KRYLOV, totals, left * right * totals))
    total = totals[:, KRYLOV : KRYLOV + 1]
    squares = jnp.sum(terms, axis=1, keepdims=True)
    length = jnp.sqrt(jnp.maximum(squares, 0.0) + epsilon)
    remainder = image[...]
    for j in range(KRYLOV):
        remainder = remainder - heights[j : j + 1, 0:BLOCK] * basis[j].astype(f32)
    remainder_out[...] = remainder
    vector_out[...] = (remainder / length).astype(bf16)
    projections_out[...] = jnp.where(lane == KRYLOV, length, totals)[0, 0 : KRYLOV + 1]
    flag_out[0] = jnp.where(squares < GUARD * total, 1, 0)[0, 0]


def shape(dims, dtype):
    return jax.ShapeDtypeStruct(dims, dtype)


def per_device(blocks, columns, margin_columns, send_lists, basis):
    devices = lax.axis_size("pitch") * lax.axis_size("span")
    square = pltpu.VMEM((LANES, LANES), f32)
    gathered = pltpu.VMEM((WIDTH, LANES), bf16)
    turned = pltpu.VMEM((LANES, WIDTH), f32)

    last, third = pack((3, 2), send_lists, blocks, basis)
    second, first = pack((1, 0), send_lists, blocks, basis)
    messages = exchange([first, second, third, last])
    chosen, gram = pl.pallas_call(
        choose_kernel,
        out_shape=[shape((LANES, SLOTS * LANES), bf16), shape((LANES - GRAM, LANES), f32)],
        in_specs=[VMEM] * 4,
        out_specs=[VMEM] * 2,
        scratch_shapes=[pltpu.VMEM((16, LANES), jnp.int32)],
        compiler_params=PARAMS,
        cost_estimate=pl.CostEstimate(flops=0, bytes_accessed=2**20, transcendentals=0),
        name="choose",
    )(blocks, columns.T, margin_columns.T, basis)
    precond, *values = pl.pallas_call(
        sweeps_kernel,
        out_shape=[shape((BLOCK, LANES), bf16)] + [shape((LIST, LANES), f32)] * 4,
        in_specs=[VMEM, VMEM, SMEM] + [VMEM] * 5,
        out_specs=[VMEM] * 5,
        scratch_shapes=[square, gathered, turned, pltpu.VMEM((LANES, 2 * LANES), bf16)],
        compiler_params=PARAMS,
        name="sweeps",
    )(blocks, chosen, send_lists, basis, *messages[::-1])
    ghosts = exchange(values)
    image, sums = pl.pallas_call(
        image_kernel,
        out_shape=[shape((F_DEV, BLOCK), f32), shape((devices, LANES), f32)],
        in_specs=[VMEM] * 9,
        out_specs=[VMEM] * 2,
        scratch_shapes=[square, gathered, turned, square],
        compiler_params=PARAMS,
        name="image",
    )(blocks, chosen, precond, *ghosts, basis, gram)
    sums = lax.all_to_all(sums.reshape(devices, 1, LANES), ("pitch", "span"), 0, 0)
    inverse_count = 1.0 / (devices * F_DEV * BLOCK)
    new_vector, projections, remainder, cancelled = pl.pallas_call(
        functools.partial(last_kernel, inverse_count),
        out_shape=[
            shape((F_DEV, BLOCK), bf16),
            shape((KRYLOV + 1,), f32),
            shape((F_DEV, BLOCK), f32),
            shape((1,), jnp.int32),
        ],
        in_specs=[VMEM] * 3,
        out_specs=[VMEM] * 3 + [SMEM],
        name="new_vector",
    )(image, basis, sums.reshape(devices, LANES))

    def summed_again(state):
        squares = lax.psum(jnp.sum(remainder * remainder), ("pitch", "span")) * inverse_count
        length = jnp.sqrt(squares + epsilon)
        return jnp.zeros_like(state[0]), (remainder / length).astype(bf16), state[2].at[KRYLOV].set(length)

    state = (cancelled, new_vector, projections)
    return lax.while_loop(lambda state: state[0][0] == 1, summed_again, state)[1:]


def solution(mesh):
    return jax.shard_map(
        per_device,
        mesh=mesh,
        in_specs=(
            P(("pitch", "span"), None, None),
            P(("pitch", "span"), None),
            P(("pitch", "span"), None),
            P(("pitch", "span"), None),
            P(None, ("pitch", "span"), None),
        ),
        out_specs=(P(("pitch", "span"), None), P()),
        check_vma=False,
    )
```
